32 devices in a mesh: section: 2 (over y), seq: 8 (over z, core), dp: 2 (over x).
Axes of the slice: x: 2, y: 2, z: 4, core: 2. Of those that a mesh axis runs over, the one named last changes fastest.
Arguments:
- mel: bfloat16 [4, 4096, 128], P('dp', 'seq'), may hold values from -6 to 6
- lengths: int32 [4], P('dp'), may hold values from 512 to 1024, as said below
- stem_weight: bfloat16 [512, 1536], P(('seq', 'dp')), may hold values from -0.25 to 0.25
- w_qkv: bfloat16 [2, 1536, 2304], P('section', ('seq', 'dp'))
- w_out: bfloat16 [2, 768, 1536], P('section', ('seq', 'dp')), may hold values from -0.21875 to 0.21875
- norm_gains: float32 [2, 2, 1536], P('section'), may hold values from 0.25 to 1.75
- conv_kernel: float32 [2, 5, 1536], P('section'), may hold values from -2.5 to 2.5
Outputs:
- arrivals: bfloat16 [2, 4, 1024, 1536], P('section', 'dp', 'seq')
The draws below stay inside these ranges and needn't reach their ends.
Inputs may be any that keep to these rules, and one draw needn't show every extreme that they name: `lengths`: every utterance keeps at least half of its 1024 frames; one utterance of each draw keeps all of them.
All inputs are finite; a program needn't handle non-finite values.
Results may differ from the reference program's by a relative error of at most 0.029.
Values may be sent and summed in bfloat16 or wider, within the bound.
No kernel may reach another device: no remote copies, remote signals or barrier semaphores. Data moves between devices by JAX's collectives and lax.ppermute only.
A program may use at most 64 MiB of HBM per device.

```python
import jax
import jax.numpy as jnp
from jax import lax

D = 1536
HEADS = 8
HD = 96
MEL = 128
STRIDE = 4
KW = 5
FRAMES_DEV = 128
FRAMES = 1024
UTTS = 4
HH = 768
N_SECTION = 2


def draw_lengths(key, part):
    key = jax.random.fold_in(key, 11)
    draw_key, pick_key = jax.random.split(key)
    drawn = jax.random.randint(draw_key, (UTTS,), FRAMES // 2, FRAMES + 1, dtype=jnp.int32)
    full_index = jax.random.randint(pick_key, (), 0, UTTS, dtype=jnp.int32)
    return jnp.where(jnp.arange(UTTS, dtype=jnp.int32) == full_index, FRAMES, drawn).astype(jnp.int32)


def draw_w_qkv(key, part):
    key = jax.random.fold_in(key, 23)
    width = HEADS * HD
    base = jax.random.normal(key, (N_SECTION, D, 3 * width), jnp.float32) * D ** (-0.5)
    return base.astype(jnp.bfloat16)


def levels(own_key, dims, shards, least, largest):
    loudness, own = 1.0, jax.random.fold_in(own_key, 6)
    for position, blocks in shards:
        steps = jnp.exp(jax.random.uniform(jax.random.fold_in(own, position), (blocks,), jnp.float32, least / len(shards), largest / len(shards)))
        loudness = loudness * jnp.repeat(steps, dims[position] // blocks).reshape([-1 if axis == position else 1 for axis in range(len(dims))])
    return loudness


def scatter_about(key, shape, scale, most, pieces=(), kind=jnp.bfloat16):
    values = jax.random.normal(key, shape, jnp.float32) * scale
    if len(pieces) > 0:
        values = levels(key, shape, pieces, -0.22, 0.18) * values
    return jnp.clip(values, min=-most, max=most).astype(kind)


def setup_inputs(seed: int = 0) -> dict:
    keys = jax.random.split(jax.random.key(seed), 8)
    mel = scatter_about(keys[0], (UTTS, STRIDE * FRAMES, MEL), 1.0, 6.0, ((0, 2), (1, 8)))
    lengths = draw_lengths(jax.random.fold_in(keys[7], 71), 0)
    stem_weight = scatter_about(keys[2], (STRIDE * MEL, D), (STRIDE * MEL) ** -0.5, 0.25, ((0, 16),))
    w_qkv = draw_w_qkv(jax.random.fold_in(keys[7], 71), 0)
    w_out = scatter_about(keys[4], (N_SECTION, HH, D), HH ** -0.5, 0.21875, ((0, 2), (1, 16)))
    norm_gains = jnp.clip(1.0 + 0.15 * jax.random.normal(keys[5], (N_SECTION, 2, D), jnp.float32), 0.25, 1.75)
    conv_kernel = scatter_about(keys[6], (N_SECTION, KW, D), KW ** -0.5, 2.5, ((0, 2),), jnp.float32)
    return {"mel": mel, "lengths": lengths, "stem_weight": stem_weight, "w_qkv": w_qkv, "w_out": w_out, "norm_gains": norm_gains, "conv_kernel": conv_kernel}


eps = 1e-05
masked_score = -1e+30

def layer_norm(value, gain):
    average = lax.optimization_barrier(jnp.mean(value, axis=-1, keepdims=True))
    centered = value - average
    variance = lax.optimization_barrier(jnp.mean(centered * centered, axis=-1, keepdims=True))
    return centered * lax.rsqrt(variance + eps) * gain

def band_attention(queries, keys_values, first_query, length, heads):
    frames = queries.shape[0]
    width = queries.shape[1]
    head_size = width // heads
    span = keys_values.shape[0]
    query_rows = queries.reshape(frames, heads, head_size).astype(jnp.float32)
    key_rows = keys_values[:, :width].reshape(span, heads, head_size).astype(jnp.float32)
    value_rows = keys_values[:, width:].reshape(span, heads, head_size).astype(jnp.float32)
    scores = jnp.einsum('qhd,khd->hqk', query_rows, key_rows) * (1.0 / head_size ** 0.5)
    query_pos = first_query + jnp.arange(frames, dtype=jnp.int32)
    key_pos = first_query - frames + jnp.arange(span, dtype=jnp.int32)
    allowed = (key_pos[None, :] >= 0) & (key_pos[None, :] < length) & (jnp.abs(query_pos[:, None] - key_pos[None, :]) <= frames)
    scores = jnp.where(allowed[None], scores, masked_score)
    highest = lax.optimization_barrier(jnp.max(scores, axis=-1, keepdims=True))
    expon = jnp.exp(scores - highest)
    probs = (expon / lax.optimization_barrier(jnp.sum(expon, axis=-1, keepdims=True))).astype(jnp.bfloat16)
    context = jnp.einsum('hqk,khd->qhd', probs.astype(jnp.float32), value_rows)
    return context.astype(jnp.bfloat16).reshape(frames, width)

def attention_all(qkv, length):
    width = HEADS * HD
    padded = jnp.pad(qkv[:, width:], ((FRAMES_DEV, FRAMES_DEV), (0, 0)))

    def one_block(block):
        first_query = (block * FRAMES_DEV).astype(jnp.int32)
        queries = lax.dynamic_slice_in_dim(qkv[:, :width], first_query, FRAMES_DEV, 0)
        nearby = lax.dynamic_slice_in_dim(padded, first_query, 3 * FRAMES_DEV, 0)
        return band_attention(queries, nearby, first_query, length, HEADS)
    blocks = lax.map(one_block, jnp.arange(FRAMES // FRAMES_DEV, dtype=jnp.int32))
    return blocks.reshape(FRAMES, width)

def apply_layer(held_input, valid, length, layer_qkv, layer_out, gains, kernel):
    stream = held_input.astype(jnp.float32)
    normed = layer_norm(stream, gains[0]).astype(jnp.bfloat16)
    qkv = jnp.dot(normed, layer_qkv, preferred_element_type=jnp.float32).astype(jnp.bfloat16)
    context = attention_all(qkv, length)
    stream = stream + jnp.dot(context, layer_out, preferred_element_type=jnp.float32)
    conv_in = (layer_norm(stream, gains[1]) * valid[:, None]).astype(jnp.bfloat16)
    rim_width = KW // 2
    padded = jnp.pad(conv_in, ((rim_width, rim_width), (0, 0)))
    conv = jnp.zeros(stream.shape, jnp.float32)
    for offset in range(KW):
        conv = conv + padded[offset:offset + FRAMES].astype(jnp.float32) * kernel[offset]
    return ((stream + jax.nn.silu(conv)) * valid[:, None]).astype(jnp.bfloat16)

def reference(mel, lengths, stem_weight, w_qkv, w_out, norm_gains, conv_kernel):
    results = []
    for utterance in range(UTTS):
        length = lengths[utterance]
        valid = (jnp.arange(FRAMES, dtype=jnp.int32) < length).astype(jnp.float32)
        grouped = mel[utterance].reshape(FRAMES, STRIDE * MEL)
        stem_out = jax.nn.silu(jnp.dot(grouped, stem_weight, preferred_element_type=jnp.float32))
        held_input = (stem_out * valid[:, None]).astype(jnp.bfloat16)
        collected = [None] * N_SECTION
        for layer in range(N_SECTION):
            held_input = apply_layer(held_input, valid, length, w_qkv[layer], w_out[layer], norm_gains[layer], conv_kernel[layer])
            collected[(layer + 1) % N_SECTION] = held_input
        results.append(jnp.stack(collected))
    return jnp.stack(results, axis=1)
```

```python
import functools

import jax
import jax.numpy as jnp
from jax import lax
from jax.experimental import pallas as pl
from jax.experimental.pallas import tpu as pltpu
from jax.sharding import PartitionSpec as P

HEADS = 8
STRIDE = 4
RIM = 8
EDGE = 8
MARGIN = 16
PARTS = 4
LOG2E = 1.4426950408889634
MIB = 1024 * 1024


eps = 1e-05
masked_score = -1e30


def from_behind(value, axis, steps):
    count = lax.axis_size(axis)
    pairs = [(source, (source + steps) % count) for source in range(count)]
    return lax.ppermute(value, axis, pairs)


def from_seq(value, steps):
    count = lax.axis_size("seq")
    pairs = [(source, source + steps) for source in range(count) if 0 <= source + steps < count]
    return lax.ppermute(value, "seq", pairs)


def ring_gather(shard, place, beside):
    count, wide = lax.axis_size("seq"), lax.axis_size("dp")
    deep = count // 2
    chips = deep * wide
    order = [(z, x) for x in range(wide) for z in (range(deep) if x % 2 == 0 else reversed(range(deep)))]

    def flat(position, core):
        z, x = order[position % chips]
        return (2 * z + core) * wide + x

    around = [(flat(p, 0), flat(p + 1, 0)) for p in range(chips)]
    around += [(flat(p, 1), flat(p - 1, 1)) for p in range(chips)]
    swap = [(i, i ^ 1) for i in range(count)]
    partner = lax.ppermute(shard, "seq", swap)
    chains = [shard, partner]
    blocks = [[shard, partner]]
    placed, chosen = (), 0
    beside = list(beside)
    arrived = beside.pop(0)((), partner)
    for step in range(1, chips // 2 + 1):
        last = step == chips // 2
        if step > 2:
            chains[0], *ready = lax.optimization_barrier((chains[0], *blocks.pop(0)))
            placed = place(ready, chosen, placed)
            chosen += len(ready)
        if step == 2 and not last:
            chains[1], *arrived = lax.optimization_barrier((chains[1], *arrived))
        if last:
            chains[0], *held = lax.optimization_barrier((chains[0], *placed, *arrived))
            placed, arrived = held[: len(placed)], held[len(placed) :]
            for send in beside:
                arrived = send(arrived, chains[0])
        came = []
        for which in range(1 if last else 2):
            chains[which] = lax.ppermute(chains[which], ("seq", "dp"), around)
            if last:
                chains[which], *arrived = lax.optimization_barrier((chains[which], *arrived))
            came += [chains[which], lax.ppermute(chains[which], "seq", swap)]
        if step == 1:
            blocks[0] += came
        else:
            blocks.append(came)
    for ready in blocks:
        placed = place(ready, chosen, placed)
        chosen += len(ready)
    return placed, arrived


def ring_owners(count, wide):
    deep = count // 2
    chips = deep * wide
    seq_index, dp_index = lax.axis_index("seq"), lax.axis_index("dp")
    core = lax.rem(seq_index, 2)
    z = lax.div(seq_index, 2)
    position = deep * dp_index + jnp.where(lax.rem(dp_index, 2) == 0, z, deep - 1 - z)

    def owner(steps, which):
        at = lax.rem(position + steps + chips, chips)
        x = lax.div(at, deep)
        z = lax.rem(at, deep)
        z = jnp.where(lax.rem(x, 2) == 0, z, deep - 1 - z)
        return (2 * z + which) * wide + x

    toward = 2 * core - 1
    owners = [owner(0, core), owner(0, 1 - core)]
    for step in range(1, chips // 2 + 1):
        owners += [owner(toward * step, core), owner(-toward * step, 1 - core)]
        if step < chips // 2:
            owners += [owner(toward * step, 1 - core), owner(-toward * step, core)]
    return owners


def silu(value):
    half = 0.5 * value
    return half + half * jnp.tanh(half)


def normalized(value, gain):
    average = jnp.mean(value, axis=-1, keepdims=True)
    centered = value - average
    variance = jnp.mean(centered * centered, axis=-1, keepdims=True)
    return centered * lax.rsqrt(variance + eps) * gain


def cut_kernel(stem_ref, qkv_ref, out_ref, shard_ref, sems):
    width = shard_ref.shape[1]
    row, copies = 0, []
    for ref in (qkv_ref, out_ref, stem_ref):
        rows = ref.shape[0]
        for part in range(ref.shape[1] // width):
            copy = pltpu.make_async_copy(
                ref.at[:, pl.ds(part * width, width)],
                shard_ref.at[pl.ds(row, rows), :],
                sems.at[len(copies)],
            )
            copy.start()
            copies.append(copy)
            row += rows
    for copy in copies:
        copy.wait()


def cut_shard(stem, qkv, out):
    width = qkv.shape[1] // 3
    rows = 3 * qkv.shape[0] + 2 * out.shape[0] + 2 * stem.shape[0]
    return pl.pallas_call(
        cut_kernel,
        out_shape=jax.ShapeDtypeStruct((rows, width), jnp.bfloat16),
        in_specs=[pl.BlockSpec(memory_space=pl.ANY)] * 3,
        out_specs=pl.BlockSpec(memory_space=pltpu.VMEM),
        scratch_shapes=[pltpu.SemaphoreType.DMA((7,))],
        compiler_params=pltpu.CompilerParams(vmem_limit_bytes=56 * MIB),
    )(stem, qkv, out)


def place_kernel(*refs, blocks, chosen, count, wide, held):
    pieces, targets = refs[:blocks], refs[blocks + held :]
    owners = ring_owners(count, wide)[chosen : chosen + blocks]
    for piece, owner in zip(pieces, owners):
        row = 0
        for target in targets:
            rows = target.shape[1] // (count * wide)
            at = pl.multiple_of(owner * rows, rows)
            for part in range(target.shape[0]):
                target[part, pl.ds(at, rows), :] = piece[row : row + rows, :]
                row += rows


def place_blocks(pieces, chosen, shapes, held=()):
    vmem = pl.BlockSpec(memory_space=pltpu.VMEM)
    return pl.pallas_call(
        functools.partial(
            place_kernel,
            blocks=len(pieces),
            chosen=chosen,
            count=lax.axis_size("seq"),
            wide=lax.axis_size("dp"),
            held=len(held),
        ),
        out_shape=[jax.ShapeDtypeStruct(shape, jnp.bfloat16) for shape in shapes],
        in_specs=[vmem] * (len(pieces) + len(held)),
        out_specs=[vmem] * len(shapes),
        input_output_aliases={len(pieces) + i: i for i in range(len(held))},
        compiler_params=pltpu.CompilerParams(vmem_limit_bytes=4 * MIB),
    )(*pieces, *held)


def group_kernel(lengths_ref, own_ref, partner_ref, got_ref, far_ref, grouped_ref, kept_ref, raw):
    span, taken = grouped_ref.shape[1], raw.shape[1]
    rows, edge = own_ref.shape[1], far_ref.shape[1]
    core = lax.rem(lax.axis_index("seq"), 2)
    low, high = edge + rows, edge + 2 * rows
    for slot in range(grouped_ref.shape[0]):
        kept_ref[slot] = lengths_ref[slot]

        def put(start, ref, at, size):
            raw[start : start + size, :] = ref[slot, at : at + size, :].astype(jnp.float32)

        put(low, own_ref, 0, rows)

        @pl.when(core == 0)
        def _():
            put(0, got_ref, 0, low)
            put(high, partner_ref, 0, rows)
            put(high + rows, far_ref, 0, edge)

        @pl.when(core == 1)
        def _():
            put(0, far_ref, 0, edge)
            put(edge, partner_ref, 0, rows)
            put(high, got_ref, edge, rows)
            put(high + rows, got_ref, 0, edge)

        for step in range(STRIDE):
            grouped_ref[slot, :, step * taken : (step + 1) * taken] = raw[
                pl.ds(step, span, stride=STRIDE), :
            ].astype(jnp.bfloat16)


def group_rows(lengths, own, partner, got, far):
    micro, rows, taken = own.shape
    raw = 3 * rows + 2 * far.shape[1]
    vmem = pl.BlockSpec(memory_space=pltpu.VMEM)
    smem = pl.BlockSpec(memory_space=pltpu.SMEM)
    return pl.pallas_call(
        group_kernel,
        out_shape=[
            jax.ShapeDtypeStruct((micro, raw // STRIDE, STRIDE * taken), own.dtype),
            jax.ShapeDtypeStruct(lengths.shape, lengths.dtype),
        ],
        in_specs=[smem] + [vmem] * 4,
        out_specs=[vmem, smem],
        scratch_shapes=[pltpu.VMEM((raw, taken), jnp.float32)],
        compiler_params=pltpu.CompilerParams(vmem_limit_bytes=4 * MIB),
    )(lengths, own, partner, got, far)


def stem_kernel(lengths_ref, grouped_ref, weight_ref, result_ref, *, slot, frames):
    span, width = grouped_ref.shape[1], weight_ref.shape[2]
    first = lax.axis_index("seq") * frames - (span - frames) // 2
    positions = first + lax.broadcasted_iota(jnp.int32, (span, 1), 0)
    valid = ((positions >= 0) & (positions < lengths_ref[slot])).astype(jnp.float32)
    for half in range(weight_ref.shape[0]):
        value = jnp.dot(grouped_ref[slot], weight_ref[half], preferred_element_type=jnp.float32)
        value = silu(value) * valid
        result_ref[:, half * width : (half + 1) * width] = value.astype(jnp.bfloat16)


def apply_stem(grouped, slot, lengths, frames, weight):
    vmem = pl.BlockSpec(memory_space=pltpu.VMEM)
    shape = (grouped.shape[1], weight.shape[0] * weight.shape[2])
    return pl.pallas_call(
        functools.partial(stem_kernel, slot=slot, frames=frames),
        out_shape=jax.ShapeDtypeStruct(shape, jnp.bfloat16),
        in_specs=[pl.BlockSpec(memory_space=pltpu.SMEM)] + [vmem] * 2,
        out_specs=vmem,
        compiler_params=pltpu.CompilerParams(vmem_limit_bytes=10 * MIB),
    )(lengths, grouped, weight)


def project(inputs, ranges, gains_ref, qkv_w, normed, queries, keys, values, middle, frames):
    model = qkv_w.shape[1]
    span, rows = normed.shape[0], queries.shape[0]
    width = middle.shape[0]
    shift = (width - rows) // 2
    row = (span - sum(end - at for at, end in ranges)) // 2
    if row > 0:
        for edge in (0, span - row):
            normed[edge : edge + row, :] = jnp.zeros((row, model), jnp.bfloat16)
    for ref, (at, end) in zip(inputs, ranges):
        while at < end:
            step = min(32, end - at) if row % 16 == 0 else min(8, end - at)
            taken = ref[at : at + step, :]
            normed[row : row + step, :] = normalized(
                taken.astype(jnp.float32), gains_ref[0:1, :]
            ).astype(jnp.bfloat16)
            low, high = max(row, frames), min(row + step, frames + width)
            if low < high:
                middle[low - frames : high - frames, :] = taken[low - row : high - row]
            row += step
            at += step
    for part, target in ((1, keys), (2, values)):
        target[...] = jnp.dot(
            normed[...], qkv_w[part], preferred_element_type=jnp.float32
        ).astype(jnp.bfloat16)
    asked = jnp.dot(
        normed[frames : frames + width, :], qkv_w[0], preferred_element_type=jnp.float32
    )
    queries[...] = asked[shift : shift + rows, :].astype(jnp.bfloat16)


def attend(
    queries, keys, values, middle, gains_ref, taps_ref, out_w, result_ref, context, stream, conv_in,
    first, length, frames, heads,
):
    width, model = out_w.shape[1], 2 * out_w.shape[2]
    head = width // heads
    rows, span = queries.shape[0], keys.shape[0]
    made = result_ref.shape[0]
    rim = (made - frames) // 2
    margin = (span - 3 * frames) // 2
    shift = (middle.shape[0] - rows) // 2
    column = 256
    query_pos = lax.broadcasted_iota(jnp.int32, (rows, span), 0) - rim - EDGE
    key_pos = lax.broadcasted_iota(jnp.int32, (rows, span), 1) - frames - margin
    allowed = (key_pos >= -first) & (key_pos < length - first)
    allowed = allowed & (jnp.abs(query_pos - key_pos) <= frames)
    bias = jnp.where(allowed, 0.0, masked_score)
    scale = LOG2E / head**0.5
    lane = lax.broadcasted_iota(jnp.int32, (rows, column), 1)

    def window_of(index):
        window = min(index * head // 128 * 128, width - column)
        low = index * head - window
        return pl.ds(window, column), (lane >= low) & (lane < low + head)

    def scores_of(index):
        cut, mine = window_of(index)
        query = queries[:, cut]
        query = jnp.where(mine, query, jnp.zeros_like(query))
        return lax.dot_general(
            query, keys[:, cut], (((1,), (1,)), ((), ())), preferred_element_type=jnp.float32
        )

    scores = scores_of(0)
    for index in range(heads):
        later = scores_of(index + 1) if index + 1 < heads else None
        cut, mine = window_of(index)
        scores = scores * scale + bias
        expon = jnp.exp2(scores - jnp.max(scores, axis=-1, keepdims=True))
        total = jnp.sum(expon, axis=-1, keepdims=True)
        mixed = jnp.dot(
            expon.astype(jnp.bfloat16), values[:, cut], preferred_element_type=jnp.float32
        ) * (1.0 / total)
        context[:, cut] = jnp.where(mine, mixed, context[:, cut])
        scores = later

    positions = first - rim - EDGE + lax.broadcasted_iota(jnp.int32, (rows, 1), 0)
    valid = ((positions >= 0) & (positions < length)).astype(jnp.float32)
    mixed = context[...].astype(jnp.bfloat16)
    for half in range(2):
        cut = pl.ds(half * width, width)
        stream[:, cut] = middle[:, cut].astype(jnp.float32)[shift : shift + rows] + jnp.dot(
            mixed, out_w[half], preferred_element_type=jnp.float32
        )

    for at in range(0, rows, 16):
        conv_in[at : at + 16, :] = (
            (normalized(stream[at : at + 16, :], gains_ref[1:2, :]) * valid[at : at + 16])
            .astype(jnp.bfloat16)
            .astype(jnp.float32)
        )

    taps = taps_ref.shape[0]
    for at in range(0, made, 16):
        conv = jnp.zeros((16, model), jnp.float32)
        for tap in range(taps):
            low = EDGE - taps // 2 + tap + at
            conv = conv + conv_in[low : low + 16, :] * taps_ref[tap : tap + 1, :]
        base = EDGE + at
        value = stream[base : base + 16, :] + silu(conv)
        result_ref[at : at + 16, :] = (value * valid[base : base + 16]).astype(jnp.bfloat16)


def layer_kernel(lengths_ref, *refs, slot, ranges, frames, heads):
    inputs, refs = refs[: len(ranges)], refs[len(ranges) :]
    gains_ref, taps_ref, qkv_w, out_w, result_ref = refs[:5]
    normed, queries, keys, values, middle, context, stream, conv_in = refs[5:]
    project(inputs, ranges, gains_ref, qkv_w, normed, queries, keys, values, middle, frames)
    attend(
        queries, keys, values, middle, gains_ref, taps_ref, out_w, result_ref, context, stream, conv_in,
        lax.axis_index("seq") * frames, lengths_ref[slot], frames, heads,
    )


def layer_buffers(frames, rim, model, width):
    span, rows, held = 3 * frames + 2 * MARGIN, frames + 2 * (rim + EDGE), frames + 2 * MARGIN
    return (
        [(span, model)],
        [(rows, width), (span, width), (span, width), (held, model)],
        [(rows, width), (rows, model), (rows, model)],
    )


def on_vmem(shapes, kind):
    return [pltpu.VMEM(shape, kind) for shape in shapes]


def apply_layer(segments, slot, lengths, frames, rim, weights, gains, kernel):
    segments, *ranges = zip(*segments)
    model, width = weights[0].shape[1:]
    normed, projected, scratch = layer_buffers(frames, rim, model, width)
    vmem = pl.BlockSpec(memory_space=pltpu.VMEM)
    body = functools.partial(
        layer_kernel, slot=slot, ranges=tuple(zip(*ranges)), frames=frames, heads=HEADS
    )
    return pl.pallas_call(
        body,
        out_shape=jax.ShapeDtypeStruct((frames + 2 * rim, model), jnp.bfloat16),
        in_specs=[pl.BlockSpec(memory_space=pltpu.SMEM)] + [vmem] * (len(segments) + 4),
        out_specs=vmem,
        scratch_shapes=on_vmem(normed + projected, jnp.bfloat16) + on_vmem(scratch, jnp.float32),
        compiler_params=pltpu.CompilerParams(vmem_limit_bytes=11 * MIB),
        cost_estimate=pl.CostEstimate(
            flops=8 * normed[0][0] * model * width + 4 * scratch[0][0] * normed[0][0] * width,
            bytes_accessed=8 * width * model,
            transcendentals=HEADS * scratch[0][0] * normed[0][0],
        ),
    )(lengths, *segments, gains, kernel, *weights)


def in_columns(weight, width):
    return jnp.stack(
        [weight[:, low : low + width] for low in range(0, weight.shape[1], width)]
    )


def gather_weights(stem, qkv, out, beside):
    devices = lax.axis_size("seq") * lax.axis_size("dp")
    width = qkv.shape[1] // 3
    if any(weight.shape[0] % 16 for weight in (stem, qkv, out)):
        whole = [lax.all_gather(w, ("seq", "dp"), axis=0, tiled=True) for w in (qkv, out, stem)]
        arrived = ()
        for send in beside:
            arrived = send(arrived, stem)
        return [in_columns(weight, width) for weight in whole], arrived
    shapes = [(w.shape[1] // width, w.shape[0] * devices, width) for w in (qkv, out, stem)]

    def place(blocks, chosen, weights):
        return place_blocks(blocks, chosen, shapes, weights)

    return ring_gather(cut_shard(stem, qkv, out), place, beside)


def edge_kernel(own_ref, partner_ref, message_ref):
    rows = own_ref.shape[1]
    edge = message_ref.shape[1] - rows
    core = lax.rem(lax.axis_index("seq"), 2)
    message_ref[:, edge:, :] = partner_ref[...]

    @pl.when(core == 0)
    def _():
        message_ref[:, :edge, :] = own_ref[:, rows - edge :, :]

    @pl.when(core == 1)
    def _():
        message_ref[:, :edge, :] = own_ref[:, :edge, :]


def far_kernel(got_ref, message_ref):
    edge = message_ref.shape[1]
    core = lax.rem(lax.axis_index("seq"), 2)

    @pl.when(core == 0)
    def _():
        message_ref[...] = got_ref[:, got_ref.shape[1] - edge :, :]

    @pl.when(core == 1)
    def _():
        message_ref[...] = got_ref[:, edge : 2 * edge, :]


def mel_beside(mel, lengths, edge):
    count = lax.axis_size("seq")
    micro, rows, taken = mel.shape
    swap = [(i, i ^ 1) for i in range(count)]
    away = [(i, i + 2) for i in range(0, count - 2, 2)] + [(i, i - 2) for i in range(3, count, 2)]

    def message(kernel, sources, size):
        vmem = pl.BlockSpec(memory_space=pltpu.VMEM)
        return pl.pallas_call(
            kernel,
            out_shape=jax.ShapeDtypeStruct((micro, size, taken), mel.dtype),
            in_specs=[vmem] * len(sources),
            out_specs=vmem,
            compiler_params=pltpu.CompilerParams(vmem_limit_bytes=4 * MIB),
        )(*sources)

    def send_near(_, after):
        own, _ = lax.optimization_barrier((mel, after))
        partner = lax.ppermute(own, "seq", swap)
        sent = message(edge_kernel, (own, partner), rows + edge)
        return own, partner, lax.ppermute(sent, "seq", away)

    def send_far(held, after):
        own, partner, got, _ = lax.optimization_barrier((*held, after))
        sent = message(far_kernel, (got,), edge)
        return group_rows(lengths, own, partner, got, lax.ppermute(sent, "seq", swap))

    return send_near, send_far


def beside_rows(rows, frames, rim, margin):
    count = frames + 2 * rim
    if rim == margin:
        return [
            (from_seq(rows, 1), 0, frames + rim),
            (rows, rim, rim + frames),
            (from_seq(rows, -1), rim, count),
        ]
    dim = rows.ndim - 2
    rows = lax.slice_in_dim(rows, rim, rim + frames, axis=dim)
    below = lax.slice_in_dim(rows, frames - margin, frames, axis=dim)
    above = lax.slice_in_dim(rows, 0, margin, axis=dim)
    return [
        (from_seq(below, 2), 0, margin),
        (from_seq(rows, 1), 0, frames),
        (rows, 0, frames),
        (from_seq(rows, -1), 0, frames),
        (from_seq(above, -2), 0, margin),
    ]


def arrive_kernel(*refs, slot, ranges):
    inputs, out_ref, sems = refs[: len(ranges)], refs[-2], refs[-1]
    sections = len(ranges)
    section = lax.axis_index("section")
    for tick, (ref, (low, high)) in enumerate(zip(inputs, ranges)):

        @pl.when(lax.rem(section + sections - 1, sections) == tick)
        def _():
            rows = (high - low) // PARTS
            copies = [
                pltpu.make_async_copy(
                    ref.at[pl.ds(low + part * rows, rows), :],
                    out_ref.at[0, slot, pl.ds(part * rows, rows), :],
                    sems.at[part],
                )
                for part in range(PARTS)
            ]
            for copy in copies:
                copy.start()
            for copy in copies:
                copy.wait()


def write_arrival(received, slot, micro, held):
    arrays, *ranges = zip(*received)
    ranges = tuple(zip(*ranges))
    shape = (1, micro, ranges[0][1] - ranges[0][0], arrays[0].shape[1])
    anywhere = pl.BlockSpec(memory_space=pl.ANY)
    return pl.pallas_call(
        functools.partial(arrive_kernel, slot=slot, ranges=ranges),
        out_shape=jax.ShapeDtypeStruct(shape, jnp.bfloat16),
        in_specs=[pl.BlockSpec(memory_space=pltpu.VMEM)] * len(arrays) + [anywhere] * len(held),
        out_specs=anywhere,
        input_output_aliases={len(arrays): 0} if held else {},
        scratch_shapes=[pltpu.SemaphoreType.DMA((PARTS,))],
        compiler_params=pltpu.CompilerParams(vmem_limit_bytes=4 * MIB),
    )(*arrays, *held)


def shards(mel, lengths, stem_weight, w_qkv, w_out, norm_gains, conv_kernel):
    sections = lax.axis_size("section")
    micro = mel.shape[0]
    frames = mel.shape[1] // STRIDE
    sends = mel_beside(mel, lengths, MARGIN * STRIDE)
    (*weights, full_stem), (grouped, lengths) = gather_weights(stem_weight, w_qkv[0], w_out[0], sends)
    gains = norm_gains[0]
    kernel = conv_kernel[0]
    received = [[] for _ in range(micro)]
    values = [None] * micro
    rim = RIM if sections > 1 else 0
    for slot in range(micro):
        if slot > 0:
            grouped, output = lax.optimization_barrier((grouped, output))
        stem = apply_stem(grouped, slot, lengths, frames, full_stem)
        segments = [(stem, 0, stem.shape[0])]
        output = apply_layer(segments, slot, lengths, frames, rim, weights, gains, kernel)
        values[slot] = from_behind(output, "section", 1)
        received[slot].append((values[slot], rim, rim + frames))
    for tick in range(1, sections):
        held = [beside_rows(value, frames, rim, RIM) for value in values]
        for slot in range(micro):
            output = apply_layer(held[slot], slot, lengths, frames, 0, weights, gains, kernel)
            values[slot] = from_behind(output, "section", 1)
            received[slot].append((values[slot], 0, frames))
        rim = 0
    arrived = ()
    for slot in range(micro):
        arrived = (write_arrival(received[slot], slot, micro, arrived),)
    return arrived[0]


def solution(mesh):
    return jax.shard_map(
        shards,
        mesh=mesh,
        in_specs=(
            P("dp", "seq", None),
            P("dp"),
            P(("seq", "dp"), None),
            P("section", ("seq", "dp"), None),
            P("section", ("seq", "dp"), None),
            P("section", None, None),
            P("section", None, None),
        ),
        out_specs=P("section", "dp", "seq", None),
        check_vma=False,
    )
```
